32 devices in a mesh: dp: 2 (over y), context: 8 (over z, core), tensor: 2 (over x).
Axes of the slice: x: 2, y: 2, z: 4, core: 2. Of those that a mesh axis runs over, the one named last changes fastest.
Arguments:
- layer_input: bfloat16 [2, 4096, 4096], P('dp', 'context', 'tensor'), may hold values from -6 to 6
- queries: bfloat16 [2, 16, 4096, 128], P('dp', 'tensor', 'context'), may hold values from -6 to 6
- key_states: bfloat16 [2, 4, 4096, 128], P('dp', 'tensor', 'context'), may hold values from -6 to 6
- value_states: bfloat16 [2, 4, 4096, 128], P('dp', 'tensor', 'context'), may hold values from -6 to 6
- out_grad: bfloat16 [2, 16, 4096, 128], P('dp', 'tensor', 'context'), may hold values from -0.0625 to 0.0625
- log_sums: bfloat16 [2, 16, 4096], P('dp', 'tensor', 'context'), may hold values from 2 to 5
- grad_dots: bfloat16 [2, 16, 4096], P('dp', 'tensor', 'context'), may hold values from -0.5 to 0.5
- doc_stretches: int32 [2, 10], P('dp'), may hold values from 1 to 4, as said below
- stretch_order: int32 [2, 128], P('dp'), may hold values from 0 to 127, as said below
- sign_vector: int32 [32, 128], P('context'), may hold values from -1 to 1, as said below
- exponents: int32 [2, 32], P('dp', 'context'), may hold values from 0 to 3
Outputs:
- rotated_grad: float32 [32, 128, 1024], P('context', 'dp', 'tensor')
The draws below stay inside these ranges and needn't reach their ends.
Inputs may be any that keep to these rules, and one draw needn't show every extreme that they name: `doc_stretches`: each row gives the lengths in units of 128 tokens of 10 documents; they sum to 32. The second document is one of the longest, exactly 4 units, and begins 512 - 128 tokens after a multiple of 512 tokens. `stretch_order`: each row is a permutation of the 128 sequence blocks. Sequence blocks d * 16 to d * 16 + 15 belong to index d of context; the 16 stored blocks of one index of context hold at most 2 blocks belonging to any one index. `sign_vector`: every entry is 1 or -1.
All inputs are finite; a program needn't handle non-finite values.
Results may differ from the reference program's by a relative error of at most 0.0075.
Values may be sent and summed in bfloat16 or wider, within the bound.
A program may use at most 64 MiB of HBM per device.

```python
import jax
import jax.numpy as jnp
from jax import lax

D = 4096
HD = 128
KVH = 4
GROUP = 4
BLK = 32
PAD = 128
HB = 128
NDOCS = 10
TOK_DEV = 512
SEQS = 2
LEN = 4096
STRETCHES = 128
SBLK = 16
CAP = 2
SPREAD = 8
DOCUNITS = 32
LONGU = 4
MAXTOK = 512
QH = 16
NBLK = 32
COLS = 1024
N_DP = 2


def draw_sign_vector(key, part):
    picked = jax.random.randint(key, (NBLK, HB), 0, 2)
    return (2 * picked - 1).astype(jnp.int32)


def doc_row(key):
    pick_key, fill_key = jax.random.split(key, 2)
    longest = LONGU
    ratio = TOK_DEV // PAD
    top_pick = (longest + 1) // ratio
    first_len = jnp.maximum(ratio * jax.random.randint(pick_key, (), 1, top_pick + 1) - 1, 1).astype(jnp.int32)
    others = NDOCS - 2
    extra = DOCUNITS - longest - first_len - others

    def add_one(index_val, counts):
        scores = jax.random.randint(jax.random.fold_in(fill_key, index_val), (others,), 0, 1 << 20) * others
        scores = scores + jnp.arange(others, dtype=jnp.int32)
        scores = jnp.where(counts < longest, scores, -1)
        chosen = lax.top_k(scores, 1)[1][0]
        return counts + (jnp.arange(others, dtype=jnp.int32) == chosen).astype(jnp.int32)
    counts = lax.fori_loop(0, extra, add_one, jnp.ones((others,), jnp.int32))
    head = jnp.stack([first_len, jnp.int32(longest)])
    return jnp.concatenate([head, counts]).astype(jnp.int32)


def draw_doc_stretches(key, part):
    keys_all = jax.random.split(key, SEQS)
    return jax.vmap(doc_row)(keys_all).astype(jnp.int32)


def shuffle_slots(sub_key):
    return jax.random.permutation(sub_key, SBLK)


def order_row(key):
    devices = STRETCHES // SBLK
    offset_key, send_key, slot_key = jax.random.split(key, 3)
    offsets = jax.random.permutation(offset_key, devices)[:SPREAD]
    send_perm = jax.vmap(shuffle_slots)(jax.random.split(send_key, devices))
    slot_perm = jax.vmap(shuffle_slots)(jax.random.split(slot_key, devices))
    source = jnp.arange(devices, dtype=jnp.int32)[:, None]
    lane = send_perm % SPREAD
    copy_index = send_perm // SPREAD
    target = (source + offsets[lane]) % devices
    landing = slot_perm[target, lane * CAP + copy_index]
    return (target * SBLK + landing).reshape(STRETCHES).astype(jnp.int32)


def draw_stretch_order(key, part):
    keys_all = jax.random.split(key, SEQS)
    return jax.vmap(order_row)(keys_all).astype(jnp.int32)


def plant(array, own_key, least, top_value):
    index_at = [jax.random.randint(jax.random.fold_in(own_key, axis), (), 0, length) for axis, length in enumerate(array.shape)]
    widest = array.shape.index(max(array.shape))
    neighbour = index_at[:widest] + [(index_at[widest] + 1) % array.shape[widest]] + index_at[widest + 1:]
    return array.at[tuple(index_at)].set(least).at[tuple(neighbour)].set(top_value)


def steps_of(key, extent, cuts, low, high):
    loudness, own = 1.0, jax.random.fold_in(key, 6)
    for dim, shards_of in cuts:
        draws = jnp.exp(jax.random.uniform(jax.random.fold_in(own, dim), (shards_of,), jnp.float32, low / len(cuts), high / len(cuts)))
        loudness = loudness * jnp.repeat(draws, extent[dim] // shards_of).reshape([-1 if axis == dim else 1 for axis in range(len(extent))])
    return loudness


def bell_draw(key, extent, scale, most, cuts=(), kind=jnp.bfloat16):
    result = jax.random.normal(key, extent, jnp.float32) * scale
    if len(cuts) > 0:
        result = steps_of(key, extent, cuts, -0.22, 0.18) * result
    return jnp.clip(result, min=-most, max=most).astype(kind)


def setup_inputs(seed: int = 0) -> dict:
    key_list = jax.random.split(jax.random.key(seed), 12)
    layer_input = bell_draw(key_list[0], (SEQS, LEN, D), 1.0, 6.0, ((0, 2), (1, 8), (2, 2)))
    queries = bell_draw(key_list[1], (SEQS, QH, LEN, HD), 1.0, 6.0, ((0, 2), (1, 2), (2, 8)))
    key_states = bell_draw(key_list[2], (SEQS, KVH, LEN, HD), 1.0, 6.0, ((0, 2), (1, 2), (2, 8)))
    value_states = bell_draw(key_list[3], (SEQS, KVH, LEN, HD), 1.0, 6.0, ((0, 2), (1, 2), (2, 8)))
    out_grad = bell_draw(key_list[4], (SEQS, QH, LEN, HD), (LEN * N_DP) ** -0.5, 0.0625, ((0, 2), (1, 2), (2, 8)))
    log_sums = jnp.clip(2.0 + 3.0 * jax.random.uniform(key_list[5], (SEQS, QH, LEN), jnp.float32) ** steps_of(key_list[5], (SEQS, QH, LEN), ((0, 2), (1, 2), (2, 8)), -0.2, 0.2), 2.0, 5.0).astype(jnp.bfloat16)
    grad_dots = bell_draw(key_list[6], (SEQS, QH, LEN), (LEN * N_DP // 64) ** -0.5, 0.5, ((0, 2), (1, 2), (2, 8)))
    doc_stretches = draw_doc_stretches(jax.random.fold_in(key_list[11], 71), 0)
    stretch_order = draw_stretch_order(jax.random.fold_in(key_list[11], 71), 0)
    sign_vector = draw_sign_vector(jax.random.fold_in(key_list[11], 71), 0)
    exponents = plant(jax.random.randint(key_list[10], (SEQS, NBLK), 0, 4), jax.random.fold_in(key_list[10], 1), 0, 3).astype(jnp.int32)
    return dict(layer_input=layer_input, queries=queries, key_states=key_states, value_states=value_states, out_grad=out_grad, log_sums=log_sums, grad_dots=grad_dots, doc_stretches=doc_stretches, stretch_order=stretch_order, sign_vector=sign_vector, exponents=exponents)


def hadamard_table(table_size):
    index_row = jnp.arange(table_size, dtype=jnp.int32)
    common = jnp.bitwise_and(index_row[:, None], index_row[None, :])
    parity = jnp.zeros((table_size, table_size), jnp.int32)
    for bit_pos in range(table_size.bit_length() - 1):
        parity = parity + jnp.bitwise_and(jnp.right_shift(common, bit_pos), 1)
    signed = 1 - 2 * jnp.bitwise_and(parity, 1)
    return signed.astype(jnp.float32) * (float(table_size) ** -0.5)


def sort_blocks(values, inverse, axis_pos):
    shape_list = list(values.shape)
    split_shape = shape_list[:axis_pos] + [STRETCHES, BLK] + shape_list[axis_pos + 1:]
    blocked = values.reshape(split_shape)
    picked = jnp.take(blocked, inverse, axis=axis_pos)
    return picked.reshape(shape_list)


def member_columns(query_seq, key_seq, value_seq, grad_seq, lse_seq, dots_seq, lengths_seq, order_seq):
    inverse = jnp.argsort(order_seq).astype(jnp.int32)
    query_sorted = sort_blocks(query_seq, inverse, 1).astype(jnp.float32)
    key_sorted = sort_blocks(key_seq, inverse, 1).astype(jnp.float32)
    value_sorted = sort_blocks(value_seq, inverse, 1).astype(jnp.float32)
    grad_sorted = sort_blocks(grad_seq, inverse, 1).astype(jnp.float32)
    lse_sorted = sort_blocks(lse_seq, inverse, 1).astype(jnp.float32)
    dots_sorted = sort_blocks(dots_seq, inverse, 1).astype(jnp.float32)
    ends = jnp.cumsum(lengths_seq).astype(jnp.int32)
    positions = jnp.arange(LEN, dtype=jnp.int32)
    token_doc = jnp.sum(((positions // PAD)[:, None] >= ends[None, :]).astype(jnp.int32), axis=1)
    window = MAXTOK // BLK
    width = MAXTOK
    scale = HD ** -0.5

    query_heads = query_sorted.reshape(KVH, GROUP, LEN, HD)
    grad_heads = grad_sorted.reshape(KVH, GROUP, LEN, HD)
    lse_heads = lse_sorted.reshape(KVH, GROUP, LEN)
    dots_heads = dots_sorted.reshape(KVH, GROUP, LEN)

    def one_head(operands):
        query_group, grad_group, lse_group, dots_group, key_head, value_head = operands

        def visit(carry, block_index):
            key_total, value_total = carry
            first_token = block_index * BLK
            window_start = jnp.clip(block_index - (window - 1), 0, STRETCHES - window) * BLK
            query_block = lax.dynamic_slice_in_dim(query_group, first_token, BLK, 1)
            grad_block = lax.dynamic_slice_in_dim(grad_group, first_token, BLK, 1)
            lse_block = lax.dynamic_slice_in_dim(lse_group, first_token, BLK, 1)
            dots_block = lax.dynamic_slice_in_dim(dots_group, first_token, BLK, 1)
            key_window = lax.dynamic_slice_in_dim(key_head, window_start, width, 0)
            value_window = lax.dynamic_slice_in_dim(value_head, window_start, width, 0)
            query_pos = lax.dynamic_slice_in_dim(positions, first_token, BLK, 0)
            query_doc = lax.dynamic_slice_in_dim(token_doc, first_token, BLK, 0)
            key_pos = lax.dynamic_slice_in_dim(positions, window_start, width, 0)
            key_doc = lax.dynamic_slice_in_dim(token_doc, window_start, width, 0)
            live = (query_doc[:, None] == key_doc[None, :]) & (key_pos[None, :] <= query_pos[:, None])
            scores = jnp.einsum('hqd,kd->hqk', query_block, key_window) * scale
            probs = jnp.where(live[None], jnp.exp(scores - lse_block[:, :, None]), 0.0)
            probs_low = lax.optimization_barrier(probs.astype(jnp.bfloat16)).astype(jnp.float32)
            value_part = jnp.einsum('hqk,hqd->kd', probs_low, grad_block)
            dprobs = jnp.einsum('hqd,kd->hqk', grad_block, value_window)
            dscores = probs * (dprobs - dots_block[:, :, None])
            dscores = lax.optimization_barrier(dscores.astype(jnp.bfloat16)).astype(jnp.float32)
            key_part = jnp.einsum('hqk,hqd->kd', dscores, query_block) * scale
            key_old = lax.dynamic_slice_in_dim(key_total, window_start, width, 0)
            value_old = lax.dynamic_slice_in_dim(value_total, window_start, width, 0)
            key_total = lax.dynamic_update_slice_in_dim(key_total, key_old + key_part, window_start, 0)
            value_total = lax.dynamic_update_slice_in_dim(value_total, value_old + value_part, window_start, 0)
            return (key_total, value_total), 0

        empty = jnp.zeros((LEN, HD), jnp.float32)
        totals, unused = lax.scan(visit, (empty, empty), jnp.arange(STRETCHES, dtype=jnp.int32))
        return jnp.stack([totals[0], totals[1]], axis=0).astype(jnp.bfloat16)

    stacked = lax.map(one_head, (query_heads, grad_heads, lse_heads, dots_heads, key_sorted, value_sorted))
    columns = jnp.transpose(stacked, (2, 0, 1, 3)).reshape(LEN, COLS)
    return columns, inverse


def reference(layer_input, queries, key_states, value_states, out_grad, log_sums, grad_dots, doc_stretches, stretch_order, sign_vector, exponents):
    had = hadamard_table(HB)
    signs_float = sign_vector.astype(jnp.float32)
    summed = jnp.zeros((NBLK, HB, COLS), jnp.float32)
    for seq_index in range(SEQS):
        columns, inverse = member_columns(queries[seq_index], key_states[seq_index], value_states[seq_index], out_grad[seq_index], log_sums[seq_index], grad_dots[seq_index], doc_stretches[seq_index], stretch_order[seq_index])
        input_sorted = sort_blocks(layer_input[seq_index], inverse, 0)
        member_grad = jnp.dot(input_sorted.T, columns, preferred_element_type=jnp.float32)
        shaped = member_grad.reshape(NBLK, HB, COLS) * signs_float[:, :, None]
        rotated = jnp.einsum('ij,bjc->bic', had, shaped, precision=lax.Precision.HIGHEST)
        factor = 1.0 / jnp.left_shift(jnp.int32(1), exponents[seq_index]).astype(jnp.float32)
        quantized = (rotated * factor[:, None, None]).astype(jnp.bfloat16)
        summed = summed + quantized.astype(jnp.float32)
    return summed
```

```python
import functools

import jax
import jax.numpy as jnp
from jax import lax
from jax.experimental import pallas as pl
from jax.experimental.pallas import tpu as pltpu
from jax.sharding import PartitionSpec as P

HD = 128
GROUP = 4
BLK = 32
PAD = 128
HB = 128
MESH = pl.DeviceIdType.MESH
STEP = 2 * PAD
VMEM_MAX = 56 * 1024 * 1024


def hadamard_signs(table_size):
    index_row = jnp.arange(table_size, dtype=jnp.int32)
    common = jnp.bitwise_and(index_row[:, None], index_row[None, :])
    parity = jnp.zeros((table_size, table_size), jnp.int32)
    for bit_pos in range(table_size.bit_length() - 1):
        parity = parity + jnp.bitwise_and(jnp.right_shift(common, bit_pos), 1)
    return (1 - 2 * jnp.bitwise_and(parity, 1)).astype(jnp.float32)


def attention_kernel(
    order_ref,
    docs_ref,
    query_ref,
    grad_ref,
    lse_ref,
    dots_ref,
    kv_ref,
    out_ref,
    kv_sorted,
    acc,
):
    groups, kv_heads, local_tokens, width = kv_ref.shape
    slots = local_tokens // BLK
    stored = groups * slots
    me = lax.axis_index("context")
    scale = HD ** (-0.5)
    rows = GROUP * BLK

    kv_sorted[:, :PAD, :] = jnp.zeros((kv_heads, PAD, width), kv_sorted.dtype)
    acc[...] = jnp.zeros_like(acc)

    @pl.loop(0, groups)
    def _(owner):
        for slot in range(slots):
            place = pl.multiple_of(PAD + order_ref[0, owner * slots + slot] * BLK, BLK)
            for head in range(kv_heads):
                kv_sorted[head, pl.ds(place, BLK), :] = kv_ref[
                    owner, head, pl.ds(slot * BLK, BLK), :
                ]

    key_iota = lax.broadcasted_iota(jnp.int32, (STEP, rows), 0)
    query_iota = lax.rem(lax.broadcasted_iota(jnp.int32, (STEP, rows), 1), BLK)

    @pl.loop(0, slots)
    def _(slot):
        block = order_ref[0, me * slots + slot]
        unit = block // (PAD // BLK)
        total = jnp.int32(0)
        start = jnp.int32(0)
        for doc in range(docs_ref.shape[1]):
            start = jnp.where(total <= unit, total, start)
            total = total + docs_ref[0, doc]
        query_pos = query_iota + block * BLK

        @pl.loop(0, (unit - start) // 2 + 1)
        def _(part):
            low_unit = unit - 1 - 2 * part
            place = pl.multiple_of((low_unit + 1) * PAD, PAD)
            key_pos = key_iota + low_unit * PAD
            live = (key_pos <= query_pos) & (key_pos >= start * PAD)
            for head in range(kv_heads):
                span = pl.ds(pl.multiple_of(slot * BLK, BLK), BLK)
                heads = pl.ds(head * GROUP, GROUP)
                query = query_ref[heads, span, :].reshape(rows, HD)
                grad = grad_ref[heads, span, :].reshape(rows, HD)
                key = kv_sorted[head, pl.ds(place, STEP), :HD]
                value = kv_sorted[head, pl.ds(place, STEP), HD:]
                lse = lse_ref[slot, head : head + 1, :]
                dots = dots_ref[slot, head : head + 1, :]
                nt = (((1,), (1,)), ((), ()))
                scores = lax.dot_general(key, query, nt, preferred_element_type=jnp.float32)
                dprobs = lax.dot_general(value, grad, nt, preferred_element_type=jnp.float32)
                probs = jnp.where(live, jnp.exp(scores * scale - lse), 0.0)
                dscores = (probs * (dprobs - dots)).astype(jnp.bfloat16)
                acc[head, pl.ds(place, STEP), :HD] += jnp.dot(
                    dscores, query, preferred_element_type=jnp.float32
                )
                acc[head, pl.ds(place, STEP), HD:] += jnp.dot(
                    probs.astype(jnp.bfloat16), grad, preferred_element_type=jnp.float32
                )

    @pl.loop(0, groups)
    def _(owner):
        for slot in range(slots):
            place = pl.multiple_of(PAD + order_ref[0, owner * slots + slot] * BLK, BLK)
            for head in range(kv_heads):
                low = head * width
                piece = acc[head, pl.ds(place, BLK), :]
                out_ref[owner, pl.ds(slot * BLK, BLK), low : low + HD] = (
                    piece[:, :HD] * scale
                ).astype(out_ref.dtype)
                out_ref[owner, pl.ds(slot * BLK, BLK), low + HD : low + width] = piece[
                    :, HD:
                ].astype(out_ref.dtype)


def attention(order, docs, queries, out_grad, lse, dots, kv_all):
    groups, kv_heads, local_tokens, width = kv_all.shape
    total = groups * local_tokens
    smem = pl.BlockSpec(memory_space=pltpu.SMEM)
    vmem = pl.BlockSpec(memory_space=pltpu.VMEM)
    return pl.pallas_call(
        attention_kernel,
        out_shape=jax.ShapeDtypeStruct(
            (groups, local_tokens, kv_heads * width), jnp.bfloat16
        ),
        in_specs=[smem, smem] + [vmem] * 5,
        out_specs=vmem,
        scratch_shapes=[
            pltpu.VMEM((kv_heads, PAD + total, width), jnp.bfloat16),
            pltpu.VMEM((kv_heads, PAD + total, width), jnp.float32),
        ],
        compiler_params=pltpu.CompilerParams(vmem_limit_bytes=VMEM_MAX),
        cost_estimate=pl.CostEstimate(
            flops=4 * 10**9, bytes_accessed=14 * 2**20, transcendentals=2**21
        ),
    )(order, docs, queries, out_grad, lse, dots, kv_all)


def ring_sum(out_at, own_at, parts):
    out_at[...] = functools.reduce(
        lambda a, b: a + b, [r[...].astype(jnp.float32) for r in [own_at] + parts]
    ).astype(out_at.dtype)


def line_stage(n, pos, device, source, target, send, recv, sems, looped):
    def copy(side, step, src):
        return pltpu.make_async_remote_copy(
            src_ref=src,
            dst_ref=recv.at[side, step],
            send_sem=sems.at[side, 0, step],
            recv_sem=sems.at[side, 1, step],
            device_id=device(1 if side == 0 else -1),
            device_id_type=MESH,
        )

    def add(out_at, own_at, parts):
        looped(out_at, own_at, parts)

    for step in range(n - 1):
        for side in (0, 1):
            place = pos if side == 0 else n - 1 - pos
            away = n - 1 - step
            dest = pos + away if side == 0 else pos - away

            @pl.when(place == 0)
            def _(side=side, step=step, dest=dest):
                copy(side, step, source(dest)).start()

            if step > 0:

                @pl.when((place >= 1) & (place <= step))
                def _(side=side, step=step, dest=dest):
                    copy(side, step - 1, send.at[side, step - 1]).wait_recv()
                    add(send.at[side, step], source(dest), [recv.at[side, step - 1]])
                    copy(side, step, send.at[side, step]).start()

    last = n - 2

    def arrived(side):
        copy(side, last, send.at[side, last]).wait_recv()

    if n > 2:

        @pl.when((pos >= 1) & (pos <= n - 2))
        def _():
            arrived(0)
            arrived(1)
            add(target, source(pos), [recv.at[0, last], recv.at[1, last]])

    @pl.when(pos == 0)
    def _():
        arrived(1)
        add(target, source(pos), [recv.at[1, last]])

    @pl.when(pos == n - 1)
    def _():
        arrived(0)
        add(target, source(pos), [recv.at[0, last]])

    for step in range(n - 1):
        for side in (0, 1):
            place = pos if side == 0 else n - 1 - pos

            @pl.when(place <= step)
            def _(side=side, step=step):
                copy(side, step, send.at[side, step]).wait_send()


def add_rows(out_at, own_at, parts):
    lead = out_at.shape[0]

    @pl.loop(0, lead)
    def _(i):
        ring_sum(out_at.at[i], own_at.at[i], [p.at[i] for p in parts])


def neighbours_barrier(lines):
    barrier = pltpu.get_barrier_semaphore()
    count = jnp.int32(0)
    for n, pos, device in lines:

        @pl.when(pos >= 1)
        def _(device=device):
            pl.semaphore_signal(barrier, inc=1, device_id=device(-1), device_id_type=MESH)

        @pl.when(pos <= n - 2)
        def _(device=device):
            pl.semaphore_signal(barrier, inc=1, device_id=device(1), device_id_type=MESH)

        count = count + jnp.where(pos >= 1, 1, 0) + jnp.where(pos <= n - 2, 1, 0)
    pl.semaphore_wait(barrier, count)


def context_lines(chips):
    me = lax.axis_index("context")
    chip, core = me // 2, lax.rem(me, 2)
    core_line = (2, core, lambda d: {"context": me + d})
    chip_line = (chips, chip, lambda d: {"context": me + 2 * d})
    return core_line, chip_line


def token_sum_kernel(part_ref, out_ref, half, send_a, recv_a, sem_a, send_b, recv_b, sem_b):
    chips = part_ref.shape[0]
    core_line, chip_line = context_lines(chips)
    neighbours_barrier([core_line, chip_line])
    line_stage(
        *core_line, lambda d: part_ref.at[:, d], half, send_a, recv_a, sem_a, add_rows
    )
    line_stage(
        *chip_line, lambda d: half.at[d], out_ref, send_b, recv_b, sem_b, add_rows
    )


def stage_scratch(n, shape):
    return [
        pltpu.VMEM((2, n - 1) + shape, jnp.bfloat16),
        pltpu.VMEM((2, n - 1) + shape, jnp.bfloat16),
        pltpu.SemaphoreType.DMA((2, 2, n - 1)),
    ]


def token_sum(parts):
    chips, cores, slabs, rows, cols = parts.shape
    vmem = pl.BlockSpec(memory_space=pltpu.VMEM)
    return pl.pallas_call(
        token_sum_kernel,
        out_shape=jax.ShapeDtypeStruct((slabs, rows, cols), jnp.bfloat16),
        in_specs=[vmem],
        out_specs=vmem,
        scratch_shapes=[pltpu.VMEM((chips, slabs, rows, cols), jnp.bfloat16)]
        + stage_scratch(cores, (chips, slabs, rows, cols))
        + stage_scratch(chips, (slabs, rows, cols)),
        compiler_params=pltpu.CompilerParams(
            collective_id=1, has_side_effects=True, vmem_limit_bytes=VMEM_MAX
        ),
        cost_estimate=pl.CostEstimate(
            flops=10**7, bytes_accessed=5 * 2**20, transcendentals=0
        ),
    )(parts)


def final_sum_kernel(
    part_ref,
    out_ref,
    half,
    quarter,
    send_a,
    recv_a,
    sem_a,
    send_b,
    recv_b,
    sem_b,
    send_c,
    recv_c,
    sem_c,
):
    chips, _, blocks, copies, rows, cols = part_ref.shape
    core_line, chip_line = context_lines(chips)
    mine = lax.axis_index("dp")
    dp_line = (copies, mine, lambda d: {"dp": mine + d})
    neighbours_barrier([core_line, dp_line, chip_line])
    line_stage(
        *core_line, lambda d: part_ref.at[:, d], half, send_a, recv_a, sem_a, add_rows
    )
    line_stage(
        *dp_line, lambda d: half.at[:, :, d], quarter, send_b, recv_b, sem_b, add_rows
    )
    line_stage(
        *chip_line, lambda d: quarter.at[d], out_ref, send_c, recv_c, sem_c, add_rows
    )


def final_sum(parts):
    chips, cores, blocks, copies, rows, cols = parts.shape
    vmem = pl.BlockSpec(memory_space=pltpu.VMEM)
    return pl.pallas_call(
        final_sum_kernel,
        out_shape=jax.ShapeDtypeStruct((blocks, rows, cols), jnp.float32),
        in_specs=[vmem],
        out_specs=vmem,
        scratch_shapes=[
            pltpu.VMEM((chips, blocks, copies, rows, cols), jnp.bfloat16),
            pltpu.VMEM((chips, blocks, rows, cols), jnp.bfloat16),
        ]
        + stage_scratch(cores, (chips, blocks, copies, rows, cols))
        + stage_scratch(copies, (chips, blocks, rows, cols))
        + stage_scratch(chips, (blocks, rows, cols)),
        compiler_params=pltpu.CompilerParams(
            collective_id=2, has_side_effects=True, vmem_limit_bytes=VMEM_MAX
        ),
        cost_estimate=pl.CostEstimate(
            flops=10**7, bytes_accessed=5 * 2**20, transcendentals=0
        ),
    )(parts)


def per_device(
    layer_input,
    queries,
    key_states,
    value_states,
    out_grad,
    log_sums,
    grad_dots,
    doc_stretches,
    stretch_order,
    sign_vector,
    exponents,
):
    heads, local_tokens = queries.shape[1], queries.shape[2]
    local_kv = key_states.shape[1]
    local_cols = 2 * local_kv * HD
    groups = lax.axis_size("context")
    copies = lax.axis_size("dp")
    chips = groups // 2
    slots = local_tokens // BLK

    kv_own = jnp.concatenate([key_states[0], value_states[0]], axis=-1)
    kv_all = lax.all_gather(kv_own, "context", axis=0, tiled=False)

    factor = 1.0 / jnp.left_shift(jnp.int32(1), exponents[0]).astype(jnp.float32)
    signs = (sign_vector.astype(jnp.float32) * factor[:, None]).astype(jnp.bfloat16)
    signs_all = lax.all_gather(signs, "context", axis=0, tiled=True)
    local_blocks = layer_input.shape[2] // HB
    signs_own = lax.dynamic_slice_in_dim(
        signs_all, lax.axis_index("tensor") * local_blocks, local_blocks, 0
    )
    turn = hadamard_signs(HB)[None] * signs_own.astype(jnp.float32)[:, None, :]
    rotated_input = (
        jnp.einsum(
            "bij,tbj->bit",
            turn.astype(jnp.bfloat16),
            layer_input[0].reshape(local_tokens, local_blocks, HB),
            preferred_element_type=jnp.float32,
        )
        * float(HB) ** (-0.5)
    ).astype(jnp.bfloat16)
    rotated_all = lax.all_gather(
        rotated_input.reshape(local_blocks * HB, local_tokens), "tensor", axis=0, tiled=True
    )

    def row_stats(stat):
        split = stat[0].astype(jnp.float32).reshape(local_kv, GROUP, slots, BLK)
        return jnp.transpose(split, (2, 0, 1, 3)).reshape(slots, local_kv, GROUP * BLK)

    parts = attention(
        stretch_order,
        doc_stretches,
        queries[0],
        out_grad[0],
        row_stats(log_sums),
        row_stats(grad_dots),
        kv_all,
    )
    slabs = 4
    kv_grad = token_sum(
        parts.reshape(chips, 2, slabs, local_tokens // slabs, local_cols)
    ).reshape(local_tokens, local_cols)
    member = jnp.dot(rotated_all, kv_grad, preferred_element_type=jnp.float32).astype(
        jnp.bfloat16
    )
    own_blocks = sign_vector.shape[0]
    return final_sum(
        member.reshape(chips, 2, own_blocks, copies, HB // copies, local_cols)
    )


def solution(mesh):
    return jax.shard_map(
        per_device,
        mesh=mesh,
        in_specs=(
            P("dp", "context", "tensor"),
            P("dp", "tensor", "context", None),
            P("dp", "tensor", "context", None),
            P("dp", "tensor", "context", None),
            P("dp", "tensor", "context", None),
            P("dp", "tensor", "context"),
            P("dp", "tensor", "context"),
            P("dp", None),
            P("dp", None),
            P("context", None),
            P("dp", "context"),
        ),
        out_specs=P("context", "dp", "tensor"),
        check_vma=False,
    )
```

```python
import functools

import jax
import jax.numpy as jnp
from jax import lax
from jax.experimental import pallas as pl
from jax.experimental.pallas import tpu as pltpu
from jax.sharding import PartitionSpec as P

HD = 128
GROUP = 4
BLK = 32
PAD = 128
HB = 128
MESH = pl.DeviceIdType.MESH
STEP = 2 * PAD
VMEM_MAX = 56 * 1024 * 1024


def hadamard_signs(table_size):
    index_row = jnp.arange(table_size, dtype=jnp.int32)
    common = jnp.bitwise_and(index_row[:, None], index_row[None, :])
    parity = jnp.zeros((table_size, table_size), jnp.int32)
    for bit_pos in range(table_size.bit_length() - 1):
        parity = parity + jnp.bitwise_and(jnp.right_shift(common, bit_pos), 1)
    return (1 - 2 * jnp.bitwise_and(parity, 1)).astype(jnp.float32)


def attention_kernel(
    order_ref,
    docs_ref,
    query_ref,
    grad_ref,
    lse_ref,
    dots_ref,
    kv_ref,
    out_ref,
    kv_sorted,
    acc,
):
    groups, kv_heads, _, width = kv_ref.shape
    local_tokens = query_ref.shape[1]
    slots = local_tokens // BLK
    me = lax.axis_index("context")
    scale = HD ** (-0.5)
    rows = GROUP * BLK

    kv_sorted[:, :PAD, :] = jnp.zeros((kv_heads, PAD, width), kv_sorted.dtype)
    acc[...] = jnp.zeros_like(acc)

    @pl.loop(0, groups)
    def _(owner):
        for slot in range(slots):
            place = pl.multiple_of(PAD + order_ref[0, owner * slots + slot] * BLK, BLK)
            for head in range(kv_heads):
                kv_sorted[head, pl.ds(place, BLK), :] = kv_ref[
                    owner, head, pl.ds(slot * BLK, BLK), :
                ]

    key_iota = lax.broadcasted_iota(jnp.int32, (STEP, rows), 0)
    query_iota = lax.rem(lax.broadcasted_iota(jnp.int32, (STEP, rows), 1), BLK)

    @pl.loop(0, slots)
    def _(slot):
        block = order_ref[0, me * slots + slot]
        unit = block // (PAD // BLK)
        total = jnp.int32(0)
        start = jnp.int32(0)
        for doc in range(docs_ref.shape[1]):
            start = jnp.where(total <= unit, total, start)
            total = total + docs_ref[0, doc]
        query_pos = query_iota + block * BLK

        @pl.loop(0, (unit - start) // 2 + 1)
        def _(part):
            low_unit = unit - 1 - 2 * part
            place = pl.multiple_of((low_unit + 1) * PAD, PAD)
            key_pos = key_iota + low_unit * PAD
            live = (key_pos <= query_pos) & (key_pos >= start * PAD)
            for head in range(kv_heads):
                span = pl.ds(pl.multiple_of(slot * BLK, BLK), BLK)
                heads = pl.ds(head * GROUP, GROUP)
                query = query_ref[heads, span, :].reshape(rows, HD)
                grad = grad_ref[heads, span, :].reshape(rows, HD)
                key = kv_sorted[head, pl.ds(place, STEP), :HD]
                value = kv_sorted[head, pl.ds(place, STEP), HD:]
                lse = lse_ref[slot, head : head + 1, :]
                dots = dots_ref[slot, head : head + 1, :]
                nt = (((1,), (1,)), ((), ()))
                scores = lax.dot_general(key, query, nt, preferred_element_type=jnp.float32)
                dprobs = lax.dot_general(value, grad, nt, preferred_element_type=jnp.float32)
                probs = jnp.where(live, jnp.exp(scores * scale - lse), 0.0)
                dscores = (probs * (dprobs - dots)).astype(jnp.bfloat16)
                acc[head, pl.ds(place, STEP), :HD] += jnp.dot(
                    dscores, query, preferred_element_type=jnp.float32
                )
                acc[head, pl.ds(place, STEP), HD:] += jnp.dot(
                    probs.astype(jnp.bfloat16), grad, preferred_element_type=jnp.float32
                )

    @pl.loop(0, groups)
    def _(owner):
        for slot in range(slots):
            place = pl.multiple_of(PAD + order_ref[0, owner * slots + slot] * BLK, BLK)
            for head in range(kv_heads):
                low = head * width
                half, row = divmod(slot * BLK, local_tokens // 2)
                piece = acc[head, pl.ds(place, BLK), :]
                out_ref[half, owner, pl.ds(row, BLK), low : low + HD] = (
                    piece[:, :HD] * scale
                ).astype(out_ref.dtype)
                out_ref[half, owner, pl.ds(row, BLK), low + HD : low + width] = piece[
                    :, HD:
                ].astype(out_ref.dtype)


def attention(order, docs, queries, out_grad, lse, dots, kv_all):
    groups, kv_heads, _, width = kv_all.shape
    local_tokens = queries.shape[1]
    total = groups * local_tokens
    smem = pl.BlockSpec(memory_space=pltpu.SMEM)
    vmem = pl.BlockSpec(memory_space=pltpu.VMEM)
    return pl.pallas_call(
        attention_kernel,
        out_shape=jax.ShapeDtypeStruct(
            (2, groups, local_tokens // 2, kv_heads * width), jnp.bfloat16
        ),
        in_specs=[smem, smem] + [vmem] * 5,
        out_specs=vmem,
        scratch_shapes=[
            pltpu.VMEM((kv_heads, PAD + total, width), jnp.bfloat16),
            pltpu.VMEM((kv_heads, PAD + total, width), jnp.float32),
        ],
        compiler_params=pltpu.CompilerParams(vmem_limit_bytes=VMEM_MAX),
        cost_estimate=pl.CostEstimate(
            flops=4 * 10**9, bytes_accessed=14 * 2**20, transcendentals=2**21
        ),
    )(order, docs, queries, out_grad, lse, dots, kv_all)


def ring_sum(out_at, own_at, parts):
    out_at[...] = functools.reduce(
        lambda a, b: a + b, [r[...].astype(jnp.float32) for r in [own_at] + parts]
    ).astype(out_at.dtype)


def line_stage(n, pos, device, source, target, send, recv, sems):
    def copy(side, step, src):
        return pltpu.make_async_remote_copy(
            src_ref=src,
            dst_ref=recv.at[side, step],
            send_sem=sems.at[side, 0, step],
            recv_sem=sems.at[side, 1, step],
            device_id=device(1 if side == 0 else -1),
            device_id_type=MESH,
        )

    def place_of(side):
        return pos if side == 0 else n - 1 - pos

    def advance(step):
        for side in (0, 1):
            place = place_of(side)
            away = n - 1 - step
            dest = pos + away if side == 0 else pos - away

            @pl.when(place == 0)
            def _(side=side, dest=dest):
                copy(side, step, source(dest)).start()

            if step > 0:

                @pl.when((place >= 1) & (place <= step))
                def _(side=side, dest=dest):
                    copy(side, step - 1, send.at[side, step - 1]).wait_recv()
                    add_rows(send.at[side, step], source(dest), [recv.at[side, step - 1]])
                    copy(side, step, send.at[side, step]).start()

    last = n - 2

    def arrived(side):
        copy(side, last, send.at[side, last]).wait_recv()

    def finish():
        if n > 2:

            @pl.when((pos >= 1) & (pos <= n - 2))
            def _():
                arrived(0)
                arrived(1)
                add_rows(target, source(pos), [recv.at[0, last], recv.at[1, last]])

        @pl.when(pos == 0)
        def _():
            arrived(1)
            add_rows(target, source(pos), [recv.at[1, last]])

        @pl.when(pos == n - 1)
        def _():
            arrived(0)
            add_rows(target, source(pos), [recv.at[0, last]])

    def drain():
        for step in range(n - 1):
            for side in (0, 1):

                @pl.when(place_of(side) <= step)
                def _(side=side, step=step):
                    copy(side, step, send.at[side, step]).wait_send()

    steps = [functools.partial(advance, step) for step in range(n - 1)] + [finish]
    return steps, drain


def interleave(*lists):
    for turn in range(max(len(steps) for steps in lists)):
        for steps in lists:
            if turn < len(steps):
                steps[turn]()


def add_rows(out_at, own_at, parts):
    lead = out_at.shape[0]

    @pl.loop(0, lead)
    def _(i):
        ring_sum(out_at.at[i], own_at.at[i], [p.at[i] for p in parts])


def neighbours_barrier(lines):
    barrier = pltpu.get_barrier_semaphore()
    count = jnp.int32(0)
    for n, pos, device in lines:

        @pl.when(pos >= 1)
        def _(device=device):
            pl.semaphore_signal(barrier, inc=1, device_id=device(-1), device_id_type=MESH)

        @pl.when(pos <= n - 2)
        def _(device=device):
            pl.semaphore_signal(barrier, inc=1, device_id=device(1), device_id_type=MESH)

        count = count + jnp.where(pos >= 1, 1, 0) + jnp.where(pos <= n - 2, 1, 0)
    pl.semaphore_wait(barrier, count)


def context_lines(chips):
    me = lax.axis_index("context")
    chip, core = me // 2, lax.rem(me, 2)
    core_line = (2, core, lambda d: {"context": me + d})
    chip_line = (chips, chip, lambda d: {"context": me + 2 * d})
    return core_line, chip_line


def token_sum_kernel(part_ref, out_ref, held, *stages):
    halves, chips = part_ref.shape[:2]
    core_line, chip_line = context_lines(chips)
    neighbours_barrier([core_line, chip_line])
    near, far, drains = [], [], []
    for i in range(halves):
        work = stages[6 * i : 6 * i + 6]
        steps, drain = line_stage(
            *core_line, lambda d, i=i: part_ref.at[i, :, d], held.at[i], *work[:3]
        )
        near.append(steps)
        drains.append(drain)
        steps, drain = line_stage(
            *chip_line, lambda d, i=i: held.at[i, d], out_ref.at[i], *work[3:]
        )
        far.append(steps)
        drains.append(drain)
    for steps in near:
        for step in steps[:-1]:
            step()
    for i in range(halves):
        near[i][-1]()
        far[i][0]()
    interleave(*[steps[1:] for steps in far])
    for drain in drains:
        drain()


def stage_scratch(n, shape):
    return [
        pltpu.VMEM((2, n - 1) + shape, jnp.bfloat16),
        pltpu.VMEM((2, n - 1) + shape, jnp.bfloat16),
        pltpu.SemaphoreType.DMA((2, 2, n - 1)),
    ]


def token_sum(parts):
    halves, chips, cores, slabs, rows, cols = parts.shape
    vmem = pl.BlockSpec(memory_space=pltpu.VMEM)
    return pl.pallas_call(
        token_sum_kernel,
        out_shape=jax.ShapeDtypeStruct((halves, slabs, rows, cols), jnp.bfloat16),
        in_specs=[vmem],
        out_specs=vmem,
        scratch_shapes=[pltpu.VMEM((halves, chips, slabs, rows, cols), jnp.bfloat16)]
        + (
            stage_scratch(cores, (chips, slabs, rows, cols))
            + stage_scratch(chips, (slabs, rows, cols))
        )
        * halves,
        compiler_params=pltpu.CompilerParams(
            collective_id=1, has_side_effects=True, vmem_limit_bytes=VMEM_MAX
        ),
        cost_estimate=pl.CostEstimate(
            flops=10**7, bytes_accessed=5 * 2**20, transcendentals=0
        ),
    )(parts)


def final_sum_kernel(part_ref, out_ref, held, over_dp, over_chips, *stages):
    chips, _, blocks, copies, rows, cols = part_ref.shape
    some = blocks // 2
    core_line, chip_line = context_lines(chips)
    mine = lax.axis_index("dp")
    dp_line = (copies, mine, lambda d: {"dp": mine + d})
    neighbours_barrier([core_line, dp_line, chip_line])
    near, drains = [], []

    def stage(index, *args):
        steps, drain = line_stage(*args, *stages[3 * index : 3 * index + 3])
        drains.append(drain)
        return steps

    for i in range(2):
        near.append(
            stage(
                i,
                *core_line,
                lambda d, i=i: part_ref.at[:, d, pl.ds(i * some, some)],
                held.at[i],
            )
        )
    a_dp = stage(2, *dp_line, lambda d: held.at[0, :, :, d], over_dp)
    a_chip = stage(3, *chip_line, lambda d: over_dp.at[d], out_ref.at[pl.ds(0, some)])
    b_chip = stage(4, *chip_line, lambda d: held.at[1, d], over_chips)
    b_dp = stage(
        5, *dp_line, lambda d: over_chips.at[:, d], out_ref.at[pl.ds(some, some)]
    )
    for steps in near:
        for step in steps[:-1]:
            step()
    near[0][-1]()
    a_dp[0]()
    near[1][-1]()
    b_chip[0]()
    interleave(b_chip[1:-1], a_dp[1:-1])
    a_dp[-1]()
    a_chip[0]()
    b_chip[-1]()
    b_dp[0]()
    interleave(a_chip[1:], b_dp[1:])
    for drain in drains:
        drain()


def final_sum(parts):
    chips, cores, blocks, copies, rows, cols = parts.shape
    some = blocks // 2
    vmem = pl.BlockSpec(memory_space=pltpu.VMEM)
    return pl.pallas_call(
        final_sum_kernel,
        out_shape=jax.ShapeDtypeStruct((blocks, rows, cols), jnp.float32),
        in_specs=[vmem],
        out_specs=vmem,
        scratch_shapes=[
            pltpu.VMEM((2, chips, some, copies, rows, cols), jnp.bfloat16),
            pltpu.VMEM((chips, some, rows, cols), jnp.bfloat16),
            pltpu.VMEM((some, copies, rows, cols), jnp.bfloat16),
        ]
        + stage_scratch(cores, (chips, some, copies, rows, cols)) * 2
        + stage_scratch(copies, (chips, some, rows, cols))
        + stage_scratch(chips, (some, rows, cols))
        + stage_scratch(chips, (some, copies, rows, cols))
        + stage_scratch(copies, (some, rows, cols)),
        compiler_params=pltpu.CompilerParams(
            collective_id=2, has_side_effects=True, vmem_limit_bytes=VMEM_MAX
        ),
        cost_estimate=pl.CostEstimate(
            flops=10**7, bytes_accessed=5 * 2**20, transcendentals=0
        ),
    )(parts)


def per_device(
    layer_input,
    queries,
    key_states,
    value_states,
    out_grad,
    log_sums,
    grad_dots,
    doc_stretches,
    stretch_order,
    sign_vector,
    exponents,
):
    heads, local_tokens = queries.shape[1], queries.shape[2]
    local_kv = key_states.shape[1]
    local_cols = 2 * local_kv * HD
    groups = lax.axis_size("context")
    copies = lax.axis_size("dp")
    chips = groups // 2
    slots = local_tokens // BLK

    own_blocks = sign_vector.shape[0]
    factor = 1.0 / jnp.left_shift(jnp.int32(1), exponents[0]).astype(jnp.float32)
    signs = (sign_vector.astype(jnp.float32) * factor[:, None]).astype(jnp.bfloat16)
    tail = jnp.pad(signs, ((0, 16 - own_blocks), (0, HD)))
    kv_own = jnp.concatenate([key_states[0], value_states[0]], axis=-1)
    kv_own = jnp.concatenate(
        [kv_own, jnp.broadcast_to(tail[None], (local_kv, 16, 2 * HD))], axis=1
    )
    kv_all = lax.all_gather(kv_own, "context", axis=0, tiled=False)
    signs_all = kv_all[:, 0, local_tokens : local_tokens + own_blocks, :HD].reshape(
        groups * own_blocks, HD
    )
    local_blocks = layer_input.shape[2] // HB
    signs_own = lax.dynamic_slice_in_dim(
        signs_all, lax.axis_index("tensor") * local_blocks, local_blocks, 0
    )
    turn = hadamard_signs(HB)[None] * signs_own.astype(jnp.float32)[:, None, :]
    rotated_input = (
        jnp.einsum(
            "bij,tbj->bit",
            turn.astype(jnp.bfloat16),
            layer_input[0].reshape(local_tokens, local_blocks, HB),
            preferred_element_type=jnp.float32,
        )
        * float(HB) ** (-0.5)
    ).astype(jnp.bfloat16)
    rotated_all = lax.all_gather(
        rotated_input.reshape(local_blocks * HB, local_tokens), "tensor", axis=0, tiled=True
    )

    def row_stats(stat):
        split = stat[0].astype(jnp.float32).reshape(local_kv, GROUP, slots, BLK)
        return jnp.transpose(split, (2, 0, 1, 3)).reshape(slots, local_kv, GROUP * BLK)

    parts = attention(
        stretch_order,
        doc_stretches,
        queries[0],
        out_grad[0],
        row_stats(log_sums),
        row_stats(grad_dots),
        kv_all,
    )
    slabs = 2
    kv_grad = token_sum(
        parts.reshape(2, chips, 2, slabs, local_tokens // slabs // 2, local_cols)
    ).reshape(local_tokens, local_cols)
    member = jnp.dot(rotated_all, kv_grad, preferred_element_type=jnp.float32).astype(
        jnp.bfloat16
    )
    return final_sum(
        member.reshape(chips, 2, own_blocks, copies, HB // copies, local_cols)
    )


def solution(mesh):
    return jax.shard_map(
        per_device,
        mesh=mesh,
        in_specs=(
            P("dp", "context", "tensor"),
            P("dp", "tensor", "context", None),
            P("dp", "tensor", "context", None),
            P("dp", "tensor", "context", None),
            P("dp", "tensor", "context", None),
            P("dp", "tensor", "context"),
            P("dp", "tensor", "context"),
            P("dp", None),
            P("dp", None),
            P("context", None),
            P("dp", "context"),
        ),
        out_specs=P("context", "dp", "tensor"),
        check_vma=False,
    )
```

```python
import functools

import jax
import jax.numpy as jnp
from jax import lax
from jax.experimental import pallas as pl
from jax.experimental.pallas import tpu as pltpu
from jax.sharding import PartitionSpec as P

HD = 128
GROUP = 4
BLK = 32
PAD = 128
HB = 128
MESH = pl.DeviceIdType.MESH
STEP = 2 * PAD
VMEM_MAX = 56 * 1024 * 1024


def hadamard_signs(table_size):
    index_row = jnp.arange(table_size, dtype=jnp.int32)
    common = jnp.bitwise_and(index_row[:, None], index_row[None, :])
    parity = jnp.zeros((table_size, table_size), jnp.int32)
    for bit_pos in range(table_size.bit_length() - 1):
        parity = parity + jnp.bitwise_and(jnp.right_shift(common, bit_pos), 1)
    return (1 - 2 * jnp.bitwise_and(parity, 1)).astype(jnp.float32)


def attention_kernel(
    order_ref,
    docs_ref,
    query_ref,
    grad_ref,
    lse_ref,
    dots_ref,
    kv_ref,
    out_ref,
    kv_sorted,
    acc,
):
    groups, kv_heads, _, width = kv_ref.shape
    local_tokens = query_ref.shape[1]
    slots = local_tokens // BLK
    me = lax.axis_index("context")
    scale = HD ** (-0.5)
    rows = GROUP * BLK

    kv_sorted[:, :PAD, :] = jnp.zeros((kv_heads, PAD, width), kv_sorted.dtype)
    acc[...] = jnp.zeros_like(acc)

    @pl.loop(0, groups)
    def _(owner):
        for slot in range(slots):
            place = pl.multiple_of(PAD + order_ref[0, owner * slots + slot] * BLK, BLK)
            for head in range(kv_heads):
                kv_sorted[head, pl.ds(place, BLK), :] = kv_ref[
                    owner, head, pl.ds(slot * BLK, BLK), :
                ]

    key_iota = lax.broadcasted_iota(jnp.int32, (STEP, rows), 0)
    query_iota = lax.rem(lax.broadcasted_iota(jnp.int32, (STEP, rows), 1), BLK)

    @pl.loop(0, slots)
    def _(slot):
        block = order_ref[0, me * slots + slot]
        unit = block // (PAD // BLK)
        total = jnp.int32(0)
        start = jnp.int32(0)
        for doc in range(docs_ref.shape[1]):
            start = jnp.where(total <= unit, total, start)
            total = total + docs_ref[0, doc]
        query_pos = query_iota + block * BLK

        @pl.loop(0, (unit - start) // 2 + 1)
        def _(part):
            low_unit = unit - 1 - 2 * part
            place = pl.multiple_of((low_unit + 1) * PAD, PAD)
            key_pos = key_iota + low_unit * PAD
            live = (key_pos <= query_pos) & (key_pos >= start * PAD)
            for head in range(kv_heads):
                span = pl.ds(pl.multiple_of(slot * BLK, BLK), BLK)
                heads = pl.ds(head * GROUP, GROUP)
                query = query_ref[heads, span, :].reshape(rows, HD)
                grad = grad_ref[heads, span, :].reshape(rows, HD)
                key = kv_sorted[head, pl.ds(place, STEP), :HD]
                value = kv_sorted[head, pl.ds(place, STEP), HD:]
                lse = lse_ref[slot, head : head + 1, :]
                dots = dots_ref[slot, head : head + 1, :]
                nt = (((1,), (1,)), ((), ()))
                scores = lax.dot_general(key, query, nt, preferred_element_type=jnp.float32)
                dprobs = lax.dot_general(value, grad, nt, preferred_element_type=jnp.float32)
                probs = jnp.where(live, jnp.exp(scores * scale - lse), 0.0)
                dscores = (probs * (dprobs - dots)).astype(jnp.bfloat16)
                acc[head, pl.ds(place, STEP), :HD] += jnp.dot(
                    dscores, query, preferred_element_type=jnp.float32
                )
                acc[head, pl.ds(place, STEP), HD:] += jnp.dot(
                    probs.astype(jnp.bfloat16), grad, preferred_element_type=jnp.float32
                )

    @pl.loop(0, groups)
    def _(owner):
        for slot in range(slots):
            place = pl.multiple_of(PAD + order_ref[0, owner * slots + slot] * BLK, BLK)
            for head in range(kv_heads):
                low = head * width
                half, row = divmod(slot * BLK, local_tokens // 4)
                piece = acc[head, pl.ds(place, BLK), :]
                out_ref[half, owner, pl.ds(row, BLK), low : low + HD] = (
                    piece[:, :HD] * scale
                ).astype(out_ref.dtype)
                out_ref[half, owner, pl.ds(row, BLK), low + HD : low + width] = piece[
                    :, HD:
                ].astype(out_ref.dtype)


def attention(order, docs, queries, out_grad, lse, dots, kv_all):
    groups, kv_heads, _, width = kv_all.shape
    local_tokens = queries.shape[1]
    total = groups * local_tokens
    smem = pl.BlockSpec(memory_space=pltpu.SMEM)
    vmem = pl.BlockSpec(memory_space=pltpu.VMEM)
    return pl.pallas_call(
        attention_kernel,
        out_shape=jax.ShapeDtypeStruct(
            (4, groups, local_tokens // 4, kv_heads * width), jnp.bfloat16
        ),
        in_specs=[smem, smem] + [vmem] * 5,
        out_specs=vmem,
        scratch_shapes=[
            pltpu.VMEM((kv_heads, PAD + total, width), jnp.bfloat16),
            pltpu.VMEM((kv_heads, PAD + total, width), jnp.float32),
        ],
        compiler_params=pltpu.CompilerParams(vmem_limit_bytes=VMEM_MAX),
        cost_estimate=pl.CostEstimate(
            flops=4 * 10**9, bytes_accessed=14 * 2**20, transcendentals=2**21
        ),
    )(order, docs, queries, out_grad, lse, dots, kv_all)


def ring_sum(out_at, own_at, parts):
    out_at[...] = functools.reduce(
        lambda a, b: a + b, [r[...].astype(jnp.float32) for r in [own_at] + parts]
    ).astype(out_at.dtype)


def line_stage(n, pos, device, source, target, send, recv, sems):
    def copy(side, step, src):
        return pltpu.make_async_remote_copy(
            src_ref=src,
            dst_ref=recv.at[side, step],
            send_sem=sems.at[side, 0, step],
            recv_sem=sems.at[side, 1, step],
            device_id=device(1 if side == 0 else -1),
            device_id_type=MESH,
        )

    def place_of(side):
        return pos if side == 0 else n - 1 - pos

    def advance(step):
        for side in (0, 1):
            place = place_of(side)
            away = n - 1 - step
            dest = pos + away if side == 0 else pos - away

            @pl.when(place == 0)
            def _(side=side, dest=dest):
                copy(side, step, source(dest)).start()

            if step > 0:

                @pl.when((place >= 1) & (place <= step))
                def _(side=side, dest=dest):
                    copy(side, step - 1, send.at[side, step - 1]).wait_recv()
                    add_rows(send.at[side, step], source(dest), [recv.at[side, step - 1]])
                    copy(side, step, send.at[side, step]).start()

    last = n - 2

    def arrived(side):
        copy(side, last, send.at[side, last]).wait_recv()

    def finish():
        if n > 2:

            @pl.when((pos >= 1) & (pos <= n - 2))
            def _():
                arrived(0)
                arrived(1)
                add_rows(target, source(pos), [recv.at[0, last], recv.at[1, last]])

        @pl.when(pos == 0)
        def _():
            arrived(1)
            add_rows(target, source(pos), [recv.at[1, last]])

        @pl.when(pos == n - 1)
        def _():
            arrived(0)
            add_rows(target, source(pos), [recv.at[0, last]])

    def drain():
        for step in range(n - 1):
            for side in (0, 1):

                @pl.when(place_of(side) <= step)
                def _(side=side, step=step):
                    copy(side, step, send.at[side, step]).wait_send()

    steps = [functools.partial(advance, step) for step in range(n - 1)] + [finish]
    return steps, drain


def interleave(*lists):
    for turn in range(max(len(steps) for steps in lists)):
        for steps in lists:
            if turn < len(steps):
                steps[turn]()


def add_rows(out_at, own_at, parts):
    lead = out_at.shape[0]

    @pl.loop(0, lead)
    def _(i):
        ring_sum(out_at.at[i], own_at.at[i], [p.at[i] for p in parts])


def neighbours_barrier(lines):
    barrier = pltpu.get_barrier_semaphore()
    count = jnp.int32(0)
    for n, pos, device in lines:

        @pl.when(pos >= 1)
        def _(device=device):
            pl.semaphore_signal(barrier, inc=1, device_id=device(-1), device_id_type=MESH)

        @pl.when(pos <= n - 2)
        def _(device=device):
            pl.semaphore_signal(barrier, inc=1, device_id=device(1), device_id_type=MESH)

        count = count + jnp.where(pos >= 1, 1, 0) + jnp.where(pos <= n - 2, 1, 0)
    pl.semaphore_wait(barrier, count)


def context_lines(chips):
    me = lax.axis_index("context")
    chip, core = me // 2, lax.rem(me, 2)
    core_line = (2, core, lambda d: {"context": me + d})
    chip_line = (chips, chip, lambda d: {"context": me + 2 * d})
    return core_line, chip_line


def token_sum_kernel(part_ref, out_ref, held, *stages):
    halves, chips = part_ref.shape[:2]
    core_line, chip_line = context_lines(chips)
    neighbours_barrier([core_line, chip_line])
    near, far, drains = [], [], []
    for i in range(halves):
        work = stages[6 * i : 6 * i + 6]
        steps, drain = line_stage(
            *core_line, lambda d, i=i: part_ref.at[i, :, d], held.at[i], *work[:3]
        )
        near.append(steps)
        drains.append(drain)
        steps, drain = line_stage(
            *chip_line, lambda d, i=i: held.at[i, d], out_ref.at[i], *work[3:]
        )
        far.append(steps)
        drains.append(drain)
    for steps in near:
        for step in steps[:-1]:
            step()
    for i in range(halves):
        near[i][-1]()
        far[i][0]()
    interleave(*[steps[1:] for steps in far])
    for drain in drains:
        drain()


def stage_scratch(n, shape):
    return [
        pltpu.VMEM((2, n - 1) + shape, jnp.bfloat16),
        pltpu.VMEM((2, n - 1) + shape, jnp.bfloat16),
        pltpu.SemaphoreType.DMA((2, 2, n - 1)),
    ]


def token_sum(parts):
    halves, chips, cores, slabs, rows, cols = parts.shape
    vmem = pl.BlockSpec(memory_space=pltpu.VMEM)
    return pl.pallas_call(
        token_sum_kernel,
        out_shape=jax.ShapeDtypeStruct((halves, slabs, rows, cols), jnp.bfloat16),
        in_specs=[vmem],
        out_specs=vmem,
        scratch_shapes=[pltpu.VMEM((halves, chips, slabs, rows, cols), jnp.bfloat16)]
        + (
            stage_scratch(cores, (chips, slabs, rows, cols))
            + stage_scratch(chips, (slabs, rows, cols))
        )
        * halves,
        compiler_params=pltpu.CompilerParams(
            collective_id=1, has_side_effects=True, vmem_limit_bytes=VMEM_MAX
        ),
        cost_estimate=pl.CostEstimate(
            flops=10**7, bytes_accessed=5 * 2**20, transcendentals=0
        ),
    )(parts)


def final_sum_kernel(part_ref, out_ref, held, over_dp, over_chips, *stages):
    chips, _, blocks, copies, rows, cols = part_ref.shape
    some = blocks // 2
    core_line, chip_line = context_lines(chips)
    mine = lax.axis_index("dp")
    dp_line = (copies, mine, lambda d: {"dp": mine + d})
    neighbours_barrier([core_line, dp_line, chip_line])
    near, drains = [], []

    def stage(index, *args):
        steps, drain = line_stage(*args, *stages[3 * index : 3 * index + 3])
        drains.append(drain)
        return steps

    for i in range(2):
        near.append(
            stage(
                i,
                *core_line,
                lambda d, i=i: part_ref.at[:, d, pl.ds(i * some, some)],
                held.at[i],
            )
        )
    a_dp = stage(2, *dp_line, lambda d: held.at[0, :, :, d], over_dp)
    a_chip = stage(3, *chip_line, lambda d: over_dp.at[d], out_ref.at[pl.ds(0, some)])
    b_chip = stage(4, *chip_line, lambda d: held.at[1, d], over_chips)
    b_dp = stage(
        5, *dp_line, lambda d: over_chips.at[:, d], out_ref.at[pl.ds(some, some)]
    )
    for steps in near:
        for step in steps[:-1]:
            step()
    near[0][-1]()
    a_dp[0]()
    near[1][-1]()
    b_chip[0]()
    interleave(b_chip[1:-1], a_dp[1:-1])
    a_dp[-1]()
    a_chip[0]()
    b_chip[-1]()
    b_dp[0]()
    interleave(a_chip[1:], b_dp[1:])
    for drain in drains:
        drain()


def final_sum(parts):
    chips, cores, blocks, copies, rows, cols = parts.shape
    some = blocks // 2
    vmem = pl.BlockSpec(memory_space=pltpu.VMEM)
    return pl.pallas_call(
        final_sum_kernel,
        out_shape=jax.ShapeDtypeStruct((blocks, rows, cols), jnp.float32),
        in_specs=[vmem],
        out_specs=vmem,
        scratch_shapes=[
            pltpu.VMEM((2, chips, some, copies, rows, cols), jnp.bfloat16),
            pltpu.VMEM((chips, some, rows, cols), jnp.bfloat16),
            pltpu.VMEM((some, copies, rows, cols), jnp.bfloat16),
        ]
        + stage_scratch(cores, (chips, some, copies, rows, cols)) * 2
        + stage_scratch(copies, (chips, some, rows, cols))
        + stage_scratch(chips, (some, rows, cols))
        + stage_scratch(chips, (some, copies, rows, cols))
        + stage_scratch(copies, (some, rows, cols)),
        compiler_params=pltpu.CompilerParams(
            collective_id=2, has_side_effects=True, vmem_limit_bytes=VMEM_MAX
        ),
        cost_estimate=pl.CostEstimate(
            flops=10**7, bytes_accessed=5 * 2**20, transcendentals=0
        ),
    )(parts)


def per_device(
    layer_input,
    queries,
    key_states,
    value_states,
    out_grad,
    log_sums,
    grad_dots,
    doc_stretches,
    stretch_order,
    sign_vector,
    exponents,
):
    heads, local_tokens = queries.shape[1], queries.shape[2]
    local_kv = key_states.shape[1]
    local_cols = 2 * local_kv * HD
    groups = lax.axis_size("context")
    copies = lax.axis_size("dp")
    chips = groups // 2
    slots = local_tokens // BLK

    own_blocks = sign_vector.shape[0]
    factor = 1.0 / jnp.left_shift(jnp.int32(1), exponents[0]).astype(jnp.float32)
    signs = (sign_vector.astype(jnp.float32) * factor[:, None]).astype(jnp.bfloat16)
    tail = jnp.pad(signs, ((0, 16 - own_blocks), (0, HD)))
    kv_own = jnp.concatenate([key_states[0], value_states[0]], axis=-1)
    kv_own = jnp.concatenate(
        [kv_own, jnp.broadcast_to(tail[None], (local_kv, 16, 2 * HD))], axis=1
    )
    kv_all = lax.all_gather(kv_own, "context", axis=0, tiled=False)
    signs_all = kv_all[:, 0, local_tokens : local_tokens + own_blocks, :HD].reshape(
        groups * own_blocks, HD
    )
    local_blocks = layer_input.shape[2] // HB
    signs_own = lax.dynamic_slice_in_dim(
        signs_all, lax.axis_index("tensor") * local_blocks, local_blocks, 0
    )
    turn = hadamard_signs(HB)[None] * signs_own.astype(jnp.float32)[:, None, :]
    rotated_input = (
        jnp.einsum(
            "bij,tbj->bit",
            turn.astype(jnp.bfloat16),
            layer_input[0].reshape(local_tokens, local_blocks, HB),
            preferred_element_type=jnp.float32,
        )
        * float(HB) ** (-0.5)
    ).astype(jnp.bfloat16)
    rotated_all = lax.all_gather(
        rotated_input.reshape(local_blocks * HB, local_tokens), "tensor", axis=0, tiled=True
    )

    def row_stats(stat):
        split = stat[0].astype(jnp.float32).reshape(local_kv, GROUP, slots, BLK)
        return jnp.transpose(split, (2, 0, 1, 3)).reshape(slots, local_kv, GROUP * BLK)

    parts = attention(
        stretch_order,
        doc_stretches,
        queries[0],
        out_grad[0],
        row_stats(log_sums),
        row_stats(grad_dots),
        kv_all,
    )
    slabs = 2
    kv_grad = token_sum(
        parts.reshape(4, chips, 2, slabs, local_tokens // slabs // 4, local_cols)
    ).reshape(local_tokens, local_cols)
    member = jnp.dot(rotated_all, kv_grad, preferred_element_type=jnp.float32).astype(
        jnp.bfloat16
    )
    return final_sum(
        member.reshape(chips, 2, own_blocks, copies, HB // copies, local_cols)
    )


def solution(mesh):
    return jax.shard_map(
        per_device,
        mesh=mesh,
        in_specs=(
            P("dp", "context", "tensor"),
            P("dp", "tensor", "context", None),
            P("dp", "tensor", "context", None),
            P("dp", "tensor", "context", None),
            P("dp", "tensor", "context", None),
            P("dp", "tensor", "context"),
            P("dp", "tensor", "context"),
            P("dp", None),
            P("dp", None),
            P("context", None),
            P("dp", "context"),
        ),
        out_specs=P("context", "dp", "tensor"),
        check_vma=False,
    )
```
